128 devices in a mesh: row: 8 (over z_hi, x), col: 8 (over y, core), rep: 2 (over z_lo).
Axes of the slice: x: 4, y: 4, z: 4 (z_hi: 2, z_lo: 2; z = z_hi * 2 + z_lo), core: 2. Of those that a mesh axis runs over, the one named last changes fastest.
Arguments:
- latents: bfloat16 [2048, 6144], P('col', ('row', 'rep')), may hold values from -6 to 6
- probe: int32 [2048, 6144], P(None, ('row', 'rep')), may hold values from 0 to 1
- w_gate: bfloat16 [6144, 16384], P(('row', 'rep'), 'col'), may hold values from -0.078125 to 0.078125
- w_up: bfloat16 [6144, 16384], P(('row', 'rep'), 'col'), may hold values from -0.078125 to 0.078125
- w_down: bfloat16 [16384, 6144], P('col', ('row', 'rep')), may hold values from -0.046875 to 0.046875
Outputs:
- grad_in: bfloat16 [2048, 6144], P('col', ('row', 'rep'))
The draws below stay inside these ranges and needn't reach their ends.
All inputs are finite; a program needn't handle non-finite values.
Results may differ from the reference program's by a relative error of at most 0.0049.
Values may be sent and summed in bfloat16 or wider, within the bound.
No kernel may reach another device: no remote copies, remote signals or barrier semaphores. Data moves between devices by JAX's collectives and lax.ppermute only.
A program may use at most 256 MiB of HBM per device.

```python
import jax
import jax.numpy as jnp

D = 6144
FF = 16384
TOKENS = 2048


def plant(drawn, rng, least, largest):
    longest = drawn.shape.index(max(drawn.shape))
    spots = []
    for shift in (0, 1):
        where = [jax.random.randint(jax.random.fold_in(rng, axis), (), 0, length) for axis, length in enumerate(drawn.shape)]
        where[longest] = (where[longest] + shift) % drawn.shape[longest]
        spots.append(tuple(where))
    return drawn.at[spots[0]].set(least).at[spots[1]].set(largest)


def block_scale(stream_key, dims, shards, smallest, top_value):
    def one(position, parts):
        draws = jax.random.uniform(jax.random.fold_in(jax.random.fold_in(stream_key, 6), position), (parts,), jnp.float32, smallest / len(shards), top_value / len(shards))
        return jnp.repeat(jnp.exp(draws), dims[position] // parts).reshape((-1,) + (1,) * (len(dims) - position - 1))

    factor_of = one(*shards[0])
    for cut in shards[1:]:
        factor_of = factor_of * one(*cut)
    return factor_of


def gaussian(own_key, dims, scale, reach, shards=(), kind=jnp.bfloat16):
    array = jax.random.normal(own_key, dims, jnp.float32) * scale
    if len(shards) > 0:
        array = block_scale(own_key, dims, shards, -0.22, 0.18) * array
    return jnp.clip(array, min=-reach, max=reach).astype(kind)


def setup_inputs(seed: int = 0) -> dict:
    key_of = jax.random.split(jax.random.key(seed), 6)
    latents = gaussian(key_of[0], (TOKENS, D), 1.0, 6.0, ((0, 8), (1, 16)))
    probe = plant(jax.random.randint(key_of[1], (TOKENS, D), 0, 2), jax.random.fold_in(key_of[1], 1), 0, 1).astype(jnp.int32)
    w_gate = gaussian(key_of[2], (D, FF), D ** -0.5, 0.078125, ((0, 16), (1, 8)))
    w_up = gaussian(key_of[3], (D, FF), D ** -0.5, 0.078125, ((0, 16), (1, 8)))
    w_down = gaussian(key_of[4], (FF, D), FF ** -0.5, 0.046875, ((0, 8), (1, 16)))
    return {"latents": latents, "probe": probe, "w_gate": w_gate, "w_up": w_up, "w_down": w_down}


def reference(latents, probe, w_gate, w_up, w_down):
    signs = (2 * probe - 1).astype(jnp.bfloat16)
    gate = jnp.dot(latents, w_gate, preferred_element_type=jnp.float32)
    up = jnp.dot(latents, w_up, preferred_element_type=jnp.float32)
    back = jnp.dot(signs, w_down.T, preferred_element_type=jnp.float32)
    sigma = jax.nn.sigmoid(gate)
    gate_slope = (back * up * sigma * (1.0 + gate * (1.0 - sigma))).astype(jnp.bfloat16)
    up_slope = (back * gate * sigma).astype(jnp.bfloat16)
    total = jnp.dot(gate_slope, w_gate.T, preferred_element_type=jnp.float32)
    total = total + jnp.dot(up_slope, w_up.T, preferred_element_type=jnp.float32)
    return total.astype(jnp.bfloat16)
```

```python
import jax
import jax.numpy as jnp
from jax import lax
from jax.sharding import PartitionSpec as P

AXES = ("row", "col", "rep")
SIDE = 4
CHUNKS = ((3, 1), (2, 0))


def place(x, y, z, c):
    return (((z // 2) * SIDE + x) * 2 * SIDE + y * 2 + c) * 2 + z % 2


def pairs(move):
    found = []
    for x in range(SIDE):
        for y in range(SIDE):
            for z in range(SIDE):
                for c in range(2):
                    nx, ny, nz, nc = move(x, y, z, c)
                    found.append((place(x, y, z, c), place(nx % SIDE, ny % SIDE, nz % SIDE, nc)))
    return found


def along(axis, by):
    def move(x, y, z, c):
        step = by if c == 0 else -by
        return (x + step * (axis == "x"), y + step * (axis == "y"), z + step * (axis == "z"), c)

    return pairs(move)


AHEAD = {axis: along(axis, 1) for axis in "xyz"}
BEHIND = {axis: along(axis, -1) for axis in "xyz"}
ACROSS = along("z", 2)
CORES = pairs(lambda x, y, z, c: (x, y, z, 1 - c))


def send(value, route):
    return lax.ppermute(value, AXES, route)


def ring_gather(value, axis):
    near = send(value, AHEAD[axis])
    far = send(near, AHEAD[axis])
    return near, send(value, BEHIND[axis]), far


def shards(latents, probe, w_gate, w_up, w_down):
    f32, bf16 = jnp.float32, jnp.bfloat16
    row, col = lax.axis_index("row"), lax.axis_index("col")
    x, z = row % SIDE, (row // SIDE) * 2 + lax.axis_index("rep")
    core = col % 2
    even = core == 0
    s = 1 - 2 * core
    tokens, features = latents.shape
    hidden = w_gate.shape[1] // SIDE
    part = tokens // SIDE

    def ordered(own, near, next_, far, axis):
        return jnp.concatenate(
            (own, jnp.where(even, near, next_), jnp.where(even, next_, near), far), axis=axis
        )

    bits = lax.dynamic_slice_in_dim(probe, col * tokens, tokens, axis=0)
    rows = jnp.stack((latents, (2 * bits - 1).astype(bf16)))
    rows = ordered(rows, *ring_gather(rows, "z"), axis=2)

    def swap_z(piece):
        return (
            piece(z),
            send(piece((z + s) % SIDE), AHEAD["z"]),
            send(piece((z - s) % SIDE), BEHIND["z"]),
            send(piece((z + 2) % SIDE), ACROSS),
        )

    def gate_up_piece(i):
        return jnp.concatenate(
            [lax.dynamic_slice_in_dim(w, i * hidden, hidden, axis=1) for w in (w_gate, w_up)], axis=1
        )

    gate_up = ordered(*swap_z(gate_up_piece), axis=0)
    down = ordered(*swap_z(lambda i: lax.dynamic_slice_in_dim(w_down, i * hidden, hidden, axis=0)), axis=1)
    both = jnp.concatenate((gate_up, send(gate_up, CORES)), axis=1)

    slots = [rows, *ring_gather(rows, "y")]
    slots = [(mine, send(mine, CORES)) for mine in slots]

    totals = {}
    for chunk in CHUNKS:

        def block(kind, i):
            return jnp.concatenate(
                [
                    lax.dynamic_slice_in_dim(slots[slot][p][kind], i * part, part, axis=0)
                    for p in range(2)
                    for slot in chunk
                ],
                axis=0,
            )

        def reduced(term):
            relay = send(term((x + 2) % SIDE).astype(bf16), AHEAD["x"])
            ahead = send((term((x + s) % SIDE) + relay).astype(bf16), AHEAD["x"])
            behind = send(term((x - s) % SIDE).astype(bf16), BEHIND["x"])
            return term(x) + ahead + behind

        gate_up_sum = reduced(lambda i: jnp.dot(block(0, i), gate_up, preferred_element_type=f32))
        back = reduced(
            lambda i: lax.dot_general(
                block(1, i), down, (((1,), (1,)), ((), ())), preferred_element_type=f32
            )
        )
        gate, up = gate_up_sum[:, :hidden], gate_up_sum[:, hidden:]
        sigma = jax.nn.sigmoid(gate)
        slopes = jnp.concatenate(
            (
                (back * up * sigma * (1.0 + gate * (1.0 - sigma))).astype(bf16),
                (back * gate * sigma).astype(bf16),
            ),
            axis=1,
        )
        half = slopes.shape[0] // 2
        slopes = jnp.concatenate((slopes[:half], send(slopes[half:], CORES)), axis=1)
        gathered = jnp.concatenate((slopes, *ring_gather(slopes, "x")), axis=0)
        out = lax.dot_general(gathered, both, (((1,), (1,)), ((), ())), preferred_element_type=f32)
        out = out.reshape(SIDE, len(chunk), part, -1)
        for n, slot in enumerate(chunk):
            totals[slot] = out[:, n]

    relay = send(totals[3].astype(bf16), BEHIND["y"])
    near = send((totals[1] + relay).astype(bf16), BEHIND["y"])
    total = totals[0] + near + send(totals[2].astype(bf16), AHEAD["y"])
    own, low, high, far = (total[:, :, n * features : (n + 1) * features] for n in range(SIDE))
    relay = send(far, AHEAD["z"])
    near = send(jnp.where(even, high, low) + relay, AHEAD["z"])
    total = own + near + send(jnp.where(even, low, high), BEHIND["z"])
    total = total.astype(bf16)

    where = [jnp.int32(0), 1 + (s + 1) // 2, jnp.int32(3), 1 + (1 - s) // 2]
    where = jnp.stack(where)
    return jnp.concatenate(
        [lax.dynamic_index_in_dim(total, where[(j - x) % SIDE], 0, keepdims=False) for j in range(SIDE)],
        axis=0,
    )


def solution(mesh):
    in_specs = (
        P("col", ("row", "rep")),
        P(None, ("row", "rep")),
        P(("row", "rep"), "col"),
        P(("row", "rep"), "col"),
        P("col", ("row", "rep")),
    )
    out_specs = P("col", ("row", "rep"))
    return jax.shard_map(shards, mesh=mesh, in_specs=in_specs, out_specs=out_specs, check_vma=False)
```

```python
import jax
import jax.numpy as jnp
from jax import lax
from jax.experimental import pallas as pl
from jax.experimental.pallas import tpu as pltpu
from jax.sharding import PartitionSpec as P

AXES = ("row", "col", "rep")
SIDE = 4
CHUNKS = ((3, 1), (2, 0))


def place(x, y, z, c):
    return (((z // 2) * SIDE + x) * 2 * SIDE + y * 2 + c) * 2 + z % 2


def pairs(move):
    found = []
    for x in range(SIDE):
        for y in range(SIDE):
            for z in range(SIDE):
                for c in range(2):
                    nx, ny, nz, nc = move(x, y, z, c)
                    found.append((place(x, y, z, c), place(nx % SIDE, ny % SIDE, nz % SIDE, nc)))
    return found


STEPS = (1, -1, 2)
SUM = [pairs(lambda x, y, z, c, n=n: (x + n * (c == 0), y, z + n * (c == 1), c)) for n in STEPS]
SWAP = [pairs(lambda x, y, z, c, n=n: (x + n * (c == 1), y, z + n * (c == 0), c)) for n in STEPS]
AHEAD = pairs(lambda x, y, z, c: (x, y + 1 - 2 * c, z, c))
BEHIND = pairs(lambda x, y, z, c: (x, y - 1 + 2 * c, z, c))
CORES = pairs(lambda x, y, z, c: (x, y, z, 1 - c))


def send(value, route):
    return lax.ppermute(value, AXES, route)


def spread(values, routes):
    return [send(v, route) for v, route in zip(values, routes)]


def after(value, *earlier):
    return lax.optimization_barrier((value, *earlier))[0]


def side_by_side(*refs):
    *ins, out = refs
    width = ins[0].shape[1]
    for k, v in enumerate(ins):
        out[:, k * width : (k + 1) * width] = v[...]


def one_above_other(*refs):
    *ins, out = refs
    for k, v in enumerate(ins):
        out[k] = v[...]


def moved(body, out_shape, grid, in_specs, out_spec, arrays, where=None):
    kernel = body if where is None else (lambda where_ref, *refs: body(*refs))
    size = sum(2 * v.size for v in arrays) + 2 * out_shape.size
    return pl.pallas_call(
        kernel,
        out_shape=out_shape,
        grid_spec=pltpu.PrefetchScalarGridSpec(
            num_scalar_prefetch=0 if where is None else 1,
            grid=grid,
            in_specs=in_specs,
            out_specs=out_spec,
        ),
        compiler_params=pltpu.CompilerParams(vmem_limit_bytes=32 * 2**20),
        cost_estimate=pl.CostEstimate(flops=0, bytes_accessed=size, transcendentals=0),
    )(*(() if where is None else (where.reshape(1),)), *arrays)


ROWS = 128


def quarter(arrays, axis, where):
    rows, cols = arrays[0].shape
    count = len(arrays)
    kind = arrays[0].dtype
    if axis == 1:
        size = cols // SIDE
        return moved(
            side_by_side,
            jax.ShapeDtypeStruct((rows, size * count), kind),
            (rows // ROWS,),
            [pl.BlockSpec((ROWS, size), lambda r, at: (r, at[0]))] * count,
            pl.BlockSpec((ROWS, size * count), lambda r, at: (r, 0)),
            arrays,
            where,
        )
    size = rows // SIDE
    blocks = size // ROWS
    return moved(
        one_above_other,
        jax.ShapeDtypeStruct((count, size, cols), kind),
        (blocks,),
        [pl.BlockSpec((ROWS, cols), lambda r, at: (at[0] * blocks + r, 0))] * count,
        pl.BlockSpec((count, ROWS, cols), lambda r, at: (0, r, 0)),
        arrays,
        where,
    ).reshape(size * count, cols)


def joined(arrays, axis):
    rows, cols = arrays[0].shape
    count = len(arrays)
    kind = arrays[0].dtype
    if axis == 1:
        return moved(
            side_by_side,
            jax.ShapeDtypeStruct((rows, cols * count), kind),
            (rows // ROWS,),
            [pl.BlockSpec((ROWS, cols), lambda r: (r, 0))] * count,
            pl.BlockSpec((ROWS, cols * count), lambda r: (r, 0)),
            arrays,
        )
    return moved(
        one_above_other,
        jax.ShapeDtypeStruct((count, rows, cols), kind),
        (rows // ROWS,),
        [pl.BlockSpec((ROWS, cols), lambda r: (r, 0))] * count,
        pl.BlockSpec((count, ROWS, cols), lambda r: (0, r, 0)),
        arrays,
    ).reshape(rows * count, cols)


def shards(latents, probe, w_gate, w_up, w_down):
    f32, bf16 = jnp.float32, jnp.bfloat16
    row, col = lax.axis_index("row"), lax.axis_index("col")
    x, z = row % SIDE, (row // SIDE) * 2 + lax.axis_index("rep")
    even = col % 2 == 0
    a, b = jnp.where(even, x, z), jnp.where(even, z, x)
    tokens, features = latents.shape
    part = tokens // SIDE

    bits = lax.dynamic_slice_in_dim(probe, col * tokens, tokens, axis=0)
    rows = jnp.stack((latents, (2 * bits - 1).astype(bf16)))
    first = spread([rows] * 3, SWAP)
    others = [send(w, CORES) for w in (w_gate, w_up)]
    others.append(send(after(w_down, *first), CORES))
    rows = jnp.concatenate((rows, *first), axis=2)
    near = send(rows, AHEAD)
    far = send(near, AHEAD)
    slots = [rows, near, send(after(rows, far), BEHIND), far]

    pieces = [quarter((w_gate, others[0], w_up, others[1]), 1, (b + n) % SIDE) for n in (0, *STEPS)]
    gate_up = joined([pieces[0], *spread(pieces[1:], SWAP)], 0)
    pieces = [quarter((w_down, others[2]), 0, (b + n) % SIDE) for n in (0, *STEPS)]
    down = joined([pieces[0], *spread([after(v, far) for v in pieces[1:]], SWAP)], 1)
    width = down.shape[0]

    def summed(terms):
        terms = [v.reshape(SIDE, part, -1) for v in terms]

        def term(step):
            blocks = [lax.dynamic_index_in_dim(v, (a + step) % SIDE, 0, keepdims=False) for v in terms]
            return jnp.concatenate(blocks, axis=0)

        got = spread([term(step).astype(bf16) for step in STEPS], SUM)
        return term(0) + got[0] + got[1] + got[2]

    totals = {}
    for chunk in CHUNKS:
        gate_up_sum = summed([jnp.dot(slots[k][0], gate_up, preferred_element_type=f32) for k in chunk])
        back = summed(
            [
                lax.dot_general(slots[k][1], down, (((1,), (1,)), ((), ())), preferred_element_type=f32)
                for k in chunk
            ]
        )
        gate, up = gate_up_sum[:, :width], gate_up_sum[:, width:]
        sigma = jax.nn.sigmoid(gate)
        slopes = jnp.concatenate(
            (
                (back * up * sigma * (1.0 + gate * (1.0 - sigma))).astype(bf16),
                (back * gate * sigma).astype(bf16),
            ),
            axis=1,
        )
        slopes = jnp.concatenate((slopes, *spread([slopes] * 3, SUM)), axis=0)
        out = lax.dot_general(slopes, gate_up, (((1,), (1,)), ((), ())), preferred_element_type=f32)
        out = out.reshape(SIDE, len(chunk), part, -1)
        for n, slot in enumerate(chunk):
            totals[slot] = out[:, n]

    relay = send(totals[3].astype(bf16), BEHIND)
    near = send((totals[1] + relay).astype(bf16), BEHIND)
    total = totals[0] + near + send(totals[2].astype(bf16), AHEAD)
    own, below, above, far = (total[:, :, n * features : (n + 1) * features] for n in range(SIDE))
    total = own
    for v in spread((above, below, far), SWAP):
        total = total + v
    total = total.astype(bf16)

    source = jnp.array([0, 2, 3, 1], jnp.int32)
    return jnp.concatenate(
        [lax.dynamic_index_in_dim(total, source[(j - a) % SIDE], 0, keepdims=False) for j in range(SIDE)],
        axis=0,
    )


def solution(mesh):
    in_specs = (
        P("col", ("row", "rep")),
        P(None, ("row", "rep")),
        P(("row", "rep"), "col"),
        P(("row", "rep"), "col"),
        P("col", ("row", "rep")),
    )
    out_specs = P("col", ("row", "rep"))
    return jax.shard_map(shards, mesh=mesh, in_specs=in_specs, out_specs=out_specs, check_vma=False)
```

```python
import jax
import jax.numpy as jnp
from jax import lax
from jax.experimental import pallas as pl
from jax.experimental.pallas import tpu as pltpu
from jax.sharding import PartitionSpec as P

AXES = ("row", "col", "rep")
SIDE = 4
CHUNKS = ((3, 1), (2, 0))


def place(x, y, z, c):
    return (((z // 2) * SIDE + x) * 2 * SIDE + y * 2 + c) * 2 + z % 2


def pairs(move):
    found = []
    for x in range(SIDE):
        for y in range(SIDE):
            for z in range(SIDE):
                for c in range(2):
                    nx, ny, nz, nc = move(x, y, z, c)
                    found.append((place(x, y, z, c), place(nx % SIDE, ny % SIDE, nz % SIDE, nc)))
    return found


STEPS = (1, -1, 2)
SUM = [pairs(lambda x, y, z, c, n=n: (x + n * (c == 0), y, z + n * (c == 1), c)) for n in STEPS]
SWAP = [pairs(lambda x, y, z, c, n=n: (x + n * (c == 1), y, z + n * (c == 0), c)) for n in STEPS]
AHEAD = pairs(lambda x, y, z, c: (x, y + 1 - 2 * c, z, c))
BEHIND = pairs(lambda x, y, z, c: (x, y - 1 + 2 * c, z, c))
HOME = [
    pairs(lambda x, y, z, c, n=n: (x + n * (c == 1), y + 1 - 2 * c, z + n * (c == 0), c)) for n in STEPS
]
CORES = pairs(lambda x, y, z, c: (x, y, z, 1 - c))


def send(value, route):
    return lax.ppermute(value, AXES, route)


def spread(values, routes):
    return [send(v, route) for v, route in zip(values, routes)]


def after(value, *earlier):
    return lax.optimization_barrier((value, *earlier))[0]


def side_by_side(*refs):
    *ins, out = refs
    width = ins[0].shape[1]
    for k, v in enumerate(ins):
        out[:, k * width : (k + 1) * width] = v[...]


def one_above_other(*refs):
    *ins, out = refs
    for k, v in enumerate(ins):
        out[k] = v[...]


def moved(body, out_shape, grid, in_specs, out_spec, arrays, where=None):
    kernel = body if where is None else (lambda where_ref, *refs: body(*refs))
    size = sum(2 * v.size for v in arrays) + 2 * out_shape.size
    return pl.pallas_call(
        kernel,
        out_shape=out_shape,
        grid_spec=pltpu.PrefetchScalarGridSpec(
            num_scalar_prefetch=0 if where is None else 1,
            grid=grid,
            in_specs=in_specs,
            out_specs=out_spec,
        ),
        compiler_params=pltpu.CompilerParams(vmem_limit_bytes=24 * 2**20),
        cost_estimate=pl.CostEstimate(flops=0, bytes_accessed=size, transcendentals=0),
    )(*(() if where is None else (where.reshape(1),)), *arrays)


ROWS = 128


def quarter(arrays, axis, where):
    rows, cols = arrays[0].shape
    count = len(arrays)
    kind = arrays[0].dtype
    if axis == 1:
        size = cols // SIDE
        return moved(
            side_by_side,
            jax.ShapeDtypeStruct((rows, size * count), kind),
            (rows // ROWS,),
            [pl.BlockSpec((ROWS, size), lambda r, at: (r, at[0]))] * count,
            pl.BlockSpec((ROWS, size * count), lambda r, at: (r, 0)),
            arrays,
            where,
        )
    size = rows // SIDE
    blocks = size // ROWS
    return moved(
        one_above_other,
        jax.ShapeDtypeStruct((count, size, cols), kind),
        (blocks,),
        [pl.BlockSpec((ROWS, cols), lambda r, at: (at[0] * blocks + r, 0))] * count,
        pl.BlockSpec((count, ROWS, cols), lambda r, at: (0, r, 0)),
        arrays,
        where,
    ).reshape(size * count, cols)


def quarters(arrays, where):
    rows, cols = arrays[0].shape
    count, size, several = len(arrays), cols // SIDE, len(where)
    kind = arrays[0].dtype

    def body(where_ref, *refs):
        for n in range(several):
            for m in range(count):
                refs[several * count + n][:, m * size : (m + 1) * size] = refs[n * count + m][...]

    return pl.pallas_call(
        body,
        out_shape=[jax.ShapeDtypeStruct((rows, size * count), kind)] * several,
        grid_spec=pltpu.PrefetchScalarGridSpec(
            num_scalar_prefetch=1,
            grid=(rows // ROWS,),
            in_specs=[
                pl.BlockSpec((ROWS, size), lambda r, at, n=n: (r, at[n])) for n in range(several) for _ in arrays
            ],
            out_specs=[pl.BlockSpec((ROWS, size * count), lambda r, at: (r, 0))] * several,
        ),
        compiler_params=pltpu.CompilerParams(vmem_limit_bytes=24 * 2**20),
        cost_estimate=pl.CostEstimate(
            flops=0, bytes_accessed=4 * several * rows * size * count, transcendentals=0
        ),
    )(where, *(list(arrays) * several))


def joined(arrays, axis):
    rows, cols = arrays[0].shape
    count = len(arrays)
    kind = arrays[0].dtype
    if axis == 1:
        return moved(
            side_by_side,
            jax.ShapeDtypeStruct((rows, cols * count), kind),
            (rows // ROWS,),
            [pl.BlockSpec((ROWS, cols), lambda r: (r, 0))] * count,
            pl.BlockSpec((ROWS, cols * count), lambda r: (r, 0)),
            arrays,
        )
    return moved(
        one_above_other,
        jax.ShapeDtypeStruct((count, rows, cols), kind),
        (rows // ROWS,),
        [pl.BlockSpec((ROWS, cols), lambda r: (r, 0))] * count,
        pl.BlockSpec((count, ROWS, cols), lambda r: (0, r, 0)),
        arrays,
    ).reshape(rows * count, cols)


def shards(latents, probe, w_gate, w_up, w_down):
    f32, bf16 = jnp.float32, jnp.bfloat16
    row, col = lax.axis_index("row"), lax.axis_index("col")
    x, z = row % SIDE, (row // SIDE) * 2 + lax.axis_index("rep")
    even = col % 2 == 0
    a, b = jnp.where(even, x, z), jnp.where(even, z, x)
    tokens, features = latents.shape
    part = tokens // SIDE

    bits = lax.dynamic_slice_in_dim(probe, col * tokens, tokens, axis=0)
    rows = jnp.stack((latents, (2 * bits - 1).astype(bf16)))
    first = spread([rows] * 3, SWAP)
    others = [send(w, CORES) for w in (w_gate, w_up)]
    others.append(send(after(w_down, *first), CORES))
    rows = jnp.concatenate((rows, *first), axis=2)
    near = send(rows, AHEAD)
    far = send(near, AHEAD)
    slots = [rows, near, send(after(rows, near), BEHIND), far]

    four = (w_gate, others[0], w_up, others[1])
    got = spread(quarters(four, (b + jnp.array(STEPS, jnp.int32)) % SIDE), SWAP)
    gate_up = joined([quarters([after(v, near) for v in four], b.reshape(1))[0], *got], 0)
    pieces = [quarter((w_down, others[2]), 0, (b + n) % SIDE) for n in (0, *STEPS)]
    down = joined([pieces[0], *spread([after(v, got[0]) for v in pieces[1:]], SWAP)], 1)
    width = down.shape[0]

    def summed(terms):
        terms = [v.reshape(SIDE, part, -1) for v in terms]

        def term(step):
            blocks = [lax.dynamic_index_in_dim(v, (a + step) % SIDE, 0, keepdims=False) for v in terms]
            return jnp.concatenate(blocks, axis=0)

        got = spread([term(step).astype(bf16) for step in STEPS], SUM)
        return term(0) + got[0] + got[1] + got[2], got[:1]

    totals, wait = {}, ()
    for chunk in CHUNKS:
        gate_up_sum, _ = summed(
            [jnp.dot(after(slots[k][0], *wait), gate_up, preferred_element_type=f32) for k in chunk]
        )
        back, wait = summed(
            [
                lax.dot_general(slots[k][1], down, (((1,), (1,)), ((), ())), preferred_element_type=f32)
                for k in chunk
            ]
        )
        gate, up = gate_up_sum[:, :width], gate_up_sum[:, width:]
        sigma = jax.nn.sigmoid(gate)
        slopes = jnp.concatenate(
            (
                (back * up * sigma * (1.0 + gate * (1.0 - sigma))).astype(bf16),
                (back * gate * sigma).astype(bf16),
            ),
            axis=1,
        )
        slopes = jnp.concatenate((slopes, *spread([slopes] * 3, SUM)), axis=0)
        out = lax.dot_general(slopes, gate_up, (((1,), (1,)), ((), ())), preferred_element_type=f32)
        out = out.reshape(SIDE, len(chunk), part, -1)
        for n, slot in enumerate(chunk):
            totals[slot] = out[:, n]

    relay = send(totals[3].astype(bf16), BEHIND)
    near = send((totals[1] + relay).astype(bf16), BEHIND)

    def cut(v):
        own, below, above, far = (v[:, :, n * features : (n + 1) * features] for n in range(SIDE))
        return own, above, below, far

    ahead = [send(v, route) for v, route in zip(cut(totals[2].astype(bf16)), (AHEAD, *HOME))]
    total, *others = cut(totals[0] + near)
    for v in spread(others, SWAP) + ahead:
        total = total + v
    total = total.astype(bf16)

    source = jnp.array([0, 2, 3, 1], jnp.int32)
    return jnp.concatenate(
        [lax.dynamic_index_in_dim(total, source[(j - a) % SIDE], 0, keepdims=False) for j in range(SIDE)],
        axis=0,
    )


def solution(mesh):
    in_specs = (
        P("col", ("row", "rep")),
        P(None, ("row", "rep")),
        P(("row", "rep"), "col"),
        P(("row", "rep"), "col"),
        P("col", ("row", "rep")),
    )
    out_specs = P("col", ("row", "rep"))
    return jax.shard_map(shards, mesh=mesh, in_specs=in_specs, out_specs=out_specs, check_vma=False)
```

```python
import jax
import jax.numpy as jnp
from jax import lax
from jax.experimental import pallas as pl
from jax.experimental.pallas import tpu as pltpu
from jax.sharding import PartitionSpec as P

AXES = ("row", "col", "rep")
SIDE = 4
CHUNKS = ((2, 1), (3, 0))


def place(x, y, z, c):
    return (((z // 2) * SIDE + x) * 2 * SIDE + y * 2 + c) * 2 + z % 2


def pairs(move):
    found = []
    for x in range(SIDE):
        for y in range(SIDE):
            for z in range(SIDE):
                for c in range(2):
                    nx, ny, nz, nc = move(x, y, z, c)
                    found.append((place(x, y, z, c), place(nx % SIDE, ny % SIDE, nz % SIDE, nc)))
    return found


STEPS = (1, -1, 2)
SUM = [pairs(lambda x, y, z, c, n=n: (x + n * (c == 0), y, z + n * (c == 1), c)) for n in STEPS]
SWAP = [pairs(lambda x, y, z, c, n=n: (x + n * (c == 1), y, z + n * (c == 0), c)) for n in STEPS]
AHEAD = pairs(lambda x, y, z, c: (x, y + 1 - 2 * c, z, c))
BEHIND = pairs(lambda x, y, z, c: (x, y - 1 + 2 * c, z, c))
HOME = [
    pairs(lambda x, y, z, c, n=n: (x + n * (c == 1), y + 2, z + n * (c == 0), c)) for n in (0, *STEPS)
]
CORES = pairs(lambda x, y, z, c: (x, y, z, 1 - c))


def send(value, route):
    return lax.ppermute(value, AXES, route)


def spread(values, routes):
    return [send(v, route) for v, route in zip(values, routes)]


def after(value, *earlier):
    return lax.optimization_barrier((value, *earlier))[0]


def side_by_side(*refs):
    *ins, out = refs
    width = ins[0].shape[1]
    for k, v in enumerate(ins):
        out[:, k * width : (k + 1) * width] = v[...]


def one_above_other(*refs):
    *ins, out = refs
    for k, v in enumerate(ins):
        out[k] = v[...]


def moved(body, out_shape, grid, in_specs, out_spec, arrays, where=None):
    kernel = body if where is None else (lambda where_ref, *refs: body(*refs))
    size = sum(2 * v.size for v in arrays) + 2 * out_shape.size
    return pl.pallas_call(
        kernel,
        out_shape=out_shape,
        grid_spec=pltpu.PrefetchScalarGridSpec(
            num_scalar_prefetch=0 if where is None else 1,
            grid=grid,
            in_specs=in_specs,
            out_specs=out_spec,
        ),
        compiler_params=pltpu.CompilerParams(vmem_limit_bytes=24 * 2**20),
        cost_estimate=pl.CostEstimate(flops=0, bytes_accessed=size, transcendentals=0),
    )(*(() if where is None else (where.reshape(1),)), *arrays)


ROWS = 128


def quarter(arrays, axis, where):
    rows, cols = arrays[0].shape
    count = len(arrays)
    kind = arrays[0].dtype
    if axis == 1:
        size = cols // SIDE
        return moved(
            side_by_side,
            jax.ShapeDtypeStruct((rows, size * count), kind),
            (rows // ROWS,),
            [pl.BlockSpec((ROWS, size), lambda r, at: (r, at[0]))] * count,
            pl.BlockSpec((ROWS, size * count), lambda r, at: (r, 0)),
            arrays,
            where,
        )
    size = rows // SIDE
    blocks = size // ROWS
    return moved(
        one_above_other,
        jax.ShapeDtypeStruct((count, size, cols), kind),
        (blocks,),
        [pl.BlockSpec((ROWS, cols), lambda r, at: (at[0] * blocks + r, 0))] * count,
        pl.BlockSpec((count, ROWS, cols), lambda r, at: (0, r, 0)),
        arrays,
        where,
    ).reshape(size * count, cols)


def quarters(arrays, where):
    rows, cols = arrays[0].shape
    count, size, several = len(arrays), cols // SIDE, len(where)
    kind = arrays[0].dtype

    def body(where_ref, *refs):
        for n in range(several):
            for m in range(count):
                refs[several * count + n][:, m * size : (m + 1) * size] = refs[n * count + m][...]

    return pl.pallas_call(
        body,
        out_shape=[jax.ShapeDtypeStruct((rows, size * count), kind)] * several,
        grid_spec=pltpu.PrefetchScalarGridSpec(
            num_scalar_prefetch=1,
            grid=(rows // ROWS,),
            in_specs=[
                pl.BlockSpec((ROWS, size), lambda r, at, n=n: (r, at[n])) for n in range(several) for _ in arrays
            ],
            out_specs=[pl.BlockSpec((ROWS, size * count), lambda r, at: (r, 0))] * several,
        ),
        compiler_params=pltpu.CompilerParams(vmem_limit_bytes=24 * 2**20),
        cost_estimate=pl.CostEstimate(
            flops=0, bytes_accessed=4 * several * rows * size * count, transcendentals=0
        ),
    )(where, *(list(arrays) * several))


def joined(arrays, axis):
    rows, cols = arrays[0].shape
    count = len(arrays)
    kind = arrays[0].dtype
    if axis == 1:
        return moved(
            side_by_side,
            jax.ShapeDtypeStruct((rows, cols * count), kind),
            (rows // ROWS,),
            [pl.BlockSpec((ROWS, cols), lambda r: (r, 0))] * count,
            pl.BlockSpec((ROWS, cols * count), lambda r: (r, 0)),
            arrays,
        )
    return moved(
        one_above_other,
        jax.ShapeDtypeStruct((count, rows, cols), kind),
        (rows // ROWS,),
        [pl.BlockSpec((ROWS, cols), lambda r: (r, 0))] * count,
        pl.BlockSpec((count, ROWS, cols), lambda r: (0, r, 0)),
        arrays,
    ).reshape(rows * count, cols)


def shards(latents, probe, w_gate, w_up, w_down):
    f32, bf16 = jnp.float32, jnp.bfloat16
    row, col = lax.axis_index("row"), lax.axis_index("col")
    x, z = row % SIDE, (row // SIDE) * 2 + lax.axis_index("rep")
    even = col % 2 == 0
    a, b = jnp.where(even, x, z), jnp.where(even, z, x)
    tokens, features = latents.shape
    part = tokens // SIDE

    bits = lax.dynamic_slice_in_dim(probe, col * tokens, tokens, axis=0)
    rows = jnp.stack((latents, (2 * bits - 1).astype(bf16)))
    first = spread([rows] * 3, SWAP)
    others = [send(w, CORES) for w in (w_gate, w_up)]
    others.append(send(after(w_down, *first), CORES))
    rows = jnp.concatenate((rows, *first), axis=2)
    near = send(rows, AHEAD)
    far = send(near, AHEAD)
    slots = [rows, near, send(after(rows, near), BEHIND), far]

    four = (w_gate, others[0], w_up, others[1])
    got = spread(quarters(four, (b + jnp.array(STEPS, jnp.int32)) % SIDE), SWAP)
    gate_up = joined([quarters([after(v, near) for v in four], b.reshape(1))[0], *got], 0)
    pieces = [quarter((w_down, others[2]), 0, (b + n) % SIDE) for n in (0, *STEPS)]
    down = joined([pieces[0], *spread([after(v, got[0]) for v in pieces[1:]], SWAP)], 1)
    width = down.shape[0]

    def summed(terms):
        terms = [v.reshape(SIDE, part, -1) for v in terms]

        def term(step):
            blocks = [lax.dynamic_index_in_dim(v, (a + step) % SIDE, 0, keepdims=False) for v in terms]
            return jnp.concatenate(blocks, axis=0)

        got = spread([term(step).astype(bf16) for step in STEPS], SUM)
        return term(0) + got[0] + got[1] + got[2], got[:1]

    totals, wait = {}, ()
    for chunk in CHUNKS:
        gate_up_sum, _ = summed(
            [jnp.dot(after(slots[k][0], *wait), gate_up, preferred_element_type=f32) for k in chunk]
        )
        back, wait = summed(
            [
                lax.dot_general(slots[k][1], down, (((1,), (1,)), ((), ())), preferred_element_type=f32)
                for k in chunk
            ]
        )
        gate, up = gate_up_sum[:, :width], gate_up_sum[:, width:]
        sigma = jax.nn.sigmoid(gate)
        slopes = jnp.concatenate(
            (
                (back * up * sigma * (1.0 + gate * (1.0 - sigma))).astype(bf16),
                (back * gate * sigma).astype(bf16),
            ),
            axis=1,
        )
        slopes = jnp.concatenate((slopes, *spread([slopes] * 3, SUM)), axis=0)
        out = lax.dot_general(slopes, gate_up, (((1,), (1,)), ((), ())), preferred_element_type=f32)
        out = out.reshape(SIDE, len(chunk), part, -1)
        for n, slot in enumerate(chunk):
            totals[slot] = out[:, n]

    def cut(v):
        own, below, above, far = (v[:, :, n * features : (n + 1) * features] for n in range(SIDE))
        return own, above, below, far

    near = send(totals[1].astype(bf16), BEHIND) + send(totals[2].astype(bf16), AHEAD).astype(f32)
    far = [send(v, route) for v, route in zip(cut(totals[3].astype(bf16)), HOME)]
    total, *others = cut(totals[0] + near)
    for v in spread(others, SWAP) + far:
        total = total + v
    total = total.astype(bf16)

    source = jnp.array([0, 2, 3, 1], jnp.int32)
    return jnp.concatenate(
        [lax.dynamic_index_in_dim(total, source[(j - a) % SIDE], 0, keepdims=False) for j in range(SIDE)],
        axis=0,
    )


def solution(mesh):
    in_specs = (
        P("col", ("row", "rep")),
        P(None, ("row", "rep")),
        P(("row", "rep"), "col"),
        P(("row", "rep"), "col"),
        P("col", ("row", "rep")),
    )
    out_specs = P("col", ("row", "rep"))
    return jax.shard_map(shards, mesh=mesh, in_specs=in_specs, out_specs=out_specs, check_vma=False)
```
